128 devices in a mesh: fsdp: 8 (over y, core), seq: 16 (over z, x).
Axes of the slice: x: 4, y: 4, z: 4, core: 2. Of those that a mesh axis runs over, the one named last changes fastest.
Arguments:
- queries: bfloat16 [8, 8192, 2048], P('fsdp', 'seq'), may hold values from -6 to 6
- keys: bfloat16 [8, 8192, 2048], P('fsdp', 'seq'), may hold values from -6 to 6
- values: bfloat16 [8, 8192, 2048], P('fsdp', 'seq'), may hold values from -6 to 6
- gates: bfloat16 [8, 8192, 2048], P('fsdp', 'seq'), may hold values from -6 to 6
- log_decay: float32 [8, 16, 8192], P('fsdp', None, 'seq'), may hold values from -1 to 0, as said below
- out_weight: bfloat16 [2048, 2048], P('fsdp'), may hold values from -0.125 to 0.125
- grad_out: bfloat16 [8, 8192, 2048], P('fsdp', 'seq'), may hold values from -6 to 6
Outputs:
- output: bfloat16 [8, 8192, 2048], P('fsdp', 'seq')
- grad_queries: bfloat16 [8, 8192, 2048], P('fsdp', 'seq')
- grad_keys: bfloat16 [8, 8192, 2048], P('fsdp', 'seq')
- grad_values: bfloat16 [8, 8192, 2048], P('fsdp', 'seq')
- grad_gates: bfloat16 [8, 8192, 2048], P('fsdp', 'seq')
- grad_weight: float32 [2048, 2048], P(('fsdp', 'seq'))
The draws below stay inside these ranges and needn't reach their ends.
Inputs may be any that keep to these rules, and one draw needn't show every extreme that they name: `log_decay`: every value is negative.
All inputs are finite; a program needn't handle non-finite values.
Results may differ from the reference program's by a relative error of at most 0.018.
Values may be sent and summed in bfloat16 or wider, within the bound.
No kernel may reach another device: no remote copies, remote signals or barrier semaphores. Data moves between devices by JAX's collectives and lax.ppermute only.
A program may use at most 256 MiB of HBM per device.

```python
import math
import jax
import jax.numpy as jnp
from jax import lax

DEVICE_ATTENDERS = 16
HEAD_DIM = 128
D = 2048
HD = 2048
TIMESTEP_COUNT = 8192
TOKENS = 65536
N_FSDP = 8


def draw_log_decay(key, part):
    key = jax.random.fold_in(key, 11)
    complete_lookup_matrix = jax.random.split(key, 5)
    slow_rate = math.log(10.0) / (4.0 * TIMESTEP_COUNT)
    fast_rate = jax.random.uniform(complete_lookup_matrix[0], (N_FSDP, DEVICE_ATTENDERS, 1), minval=1.0 / 50.0, maxval=1.0 / 30.0)
    share = 0.5
    slow = jax.random.uniform(complete_lookup_matrix[1], (N_FSDP, DEVICE_ATTENDERS, 1)) < share
    starting_level = jnp.where(slow, slow_rate, fast_rate)
    random_perturbation = jnp.exp(jax.random.uniform(complete_lookup_matrix[2], (N_FSDP, DEVICE_ATTENDERS, TIMESTEP_COUNT), minval=-0.7, maxval=0.7))
    marked_indices = jax.random.uniform(complete_lookup_matrix[3], (N_FSDP, 1, TIMESTEP_COUNT)) < 3.0 / TIMESTEP_COUNT
    spike_magnitude = jax.random.uniform(complete_lookup_matrix[4], (N_FSDP, DEVICE_ATTENDERS, TIMESTEP_COUNT), minval=0.22, maxval=0.69)
    return -(starting_level * random_perturbation + jnp.where(marked_indices, spike_magnitude, 0.0))


def block_levels(stream_key, shape, shards, smallest, largest):
    level = 1.0
    for position, parts in shards:
        heights = jax.random.uniform(jax.random.fold_in(jax.random.fold_in(stream_key, 6), position), (parts,), jnp.float32, smallest / len(shards), largest / len(shards))
        level = level * jnp.repeat(jnp.exp(heights), shape[position] // parts).reshape((-1,) + (1,) * (len(shape) - 1 - position))
    return level


def noise(rng, dims, spread, bound, cuts=(), held_as=jnp.bfloat16):
    entries = spread * jax.random.normal(rng, dims, jnp.float32)
    if cuts:
        entries = entries * block_levels(rng, dims, cuts, -0.22, 0.18)
    return jnp.clip(entries, -bound, bound).astype(held_as)


def setup_inputs(seed: int = 0) -> dict:
    arg_keys = jax.random.split(jax.random.key(seed), 8)
    return {
        "queries": noise(arg_keys[0], (N_FSDP, TIMESTEP_COUNT, HD), 1.0, 6.0, ((0, 8), (1, 16))),
        "keys": noise(arg_keys[1], (N_FSDP, TIMESTEP_COUNT, HD), 1.0, 6.0, ((0, 8), (1, 16))),
        "values": noise(arg_keys[2], (N_FSDP, TIMESTEP_COUNT, HD), 1.0, 6.0, ((0, 8), (1, 16))),
        "gates": noise(arg_keys[3], (N_FSDP, TIMESTEP_COUNT, HD), 1.0, 6.0, ((0, 8), (1, 16))),
        "log_decay": draw_log_decay(jax.random.fold_in(arg_keys[7], 71), 0),
        "out_weight": noise(arg_keys[5], (HD, D), HD ** -0.5, 0.125, ((0, 8),)),
        "grad_out": noise(arg_keys[6], (N_FSDP, TIMESTEP_COUNT, D), 1.0, 6.0, ((0, 8), (1, 16))),
    }


HIGH = lax.Precision.HIGHEST

def local_output(query_f, key_f, value_f, cumul, state):
    length = query_f.shape[0]
    scores = jnp.einsum('thd,shd->hts', query_f, key_f, precision=HIGH)
    gap = cumul[:, :, None] - cumul[:, None, :]
    causal = lax.broadcasted_iota(jnp.int32, (length, length), 0) >= lax.broadcasted_iota(jnp.int32, (length, length), 1)
    weights = jnp.where(causal, jnp.exp(jnp.where(causal, gap, 0.0)), 0.0)
    inner = jnp.einsum('hts,she->the', weights * scores, value_f, precision=HIGH)
    carried = jnp.einsum('thd,hde->the', query_f, state, precision=HIGH) * jnp.exp(cumul).T[:, :, None]
    return inner + carried

def advance_state(key_f, value_f, cumul, state):
    ending = cumul[:, -1]
    tail = jnp.exp(ending[:, None] - cumul)
    return jnp.exp(ending)[:, None, None] * state + jnp.einsum('shd,hs,she->hde', key_f, tail, value_f, precision=HIGH)

def normalize(mixed, gate_f):
    length = mixed.shape[0]
    scaled = mixed * lax.rsqrt(lax.optimization_barrier(jnp.mean(mixed * mixed, axis=-1, keepdims=True)) + 1e-05)
    return scaled.reshape(length, -1) * jax.nn.silu(gate_f)

def sequence_hidden(query_f, key_f, value_f, gate_f, decay):
    block = math.gcd(512, TIMESTEP_COUNT)
    blocks = TIMESTEP_COUNT // block
    qb = query_f.reshape(blocks, block, DEVICE_ATTENDERS, HEAD_DIM)
    kb = key_f.reshape(blocks, block, DEVICE_ATTENDERS, HEAD_DIM)
    vb = value_f.reshape(blocks, block, DEVICE_ATTENDERS, HEAD_DIM)
    ab = decay.reshape(DEVICE_ATTENDERS, blocks, block).transpose(1, 0, 2)

    def step(state, pieces):
        q_part, k_part, v_part, a_part = pieces
        cumul = jnp.cumsum(a_part, axis=1)
        mixed = local_output(q_part, k_part, v_part, cumul, state)
        return (advance_state(k_part, v_part, cumul, state), mixed)
    start = jnp.zeros((DEVICE_ATTENDERS, HEAD_DIM, HEAD_DIM), jnp.float32)
    _, mixed = lax.scan(step, start, (qb, kb, vb, ab))
    return normalize(mixed.reshape(TIMESTEP_COUNT, DEVICE_ATTENDERS, HEAD_DIM), gate_f)

def reference(queries, keys, values, gates, log_decay, out_weight, grad_out):

    def one_sequence(pieces):
        q_seq, k_seq, v_seq, g_seq, decay, cotangent = pieces
        inputs = (q_seq.astype(jnp.float32).reshape(TIMESTEP_COUNT, DEVICE_ATTENDERS, HEAD_DIM), k_seq.astype(jnp.float32).reshape(TIMESTEP_COUNT, DEVICE_ATTENDERS, HEAD_DIM), v_seq.astype(jnp.float32).reshape(TIMESTEP_COUNT, DEVICE_ATTENDERS, HEAD_DIM), g_seq.astype(jnp.float32))

        def forward(query_f, key_f, value_f, gate_f):
            return sequence_hidden(query_f, key_f, value_f, gate_f, decay)
        hidden_f, pull = jax.vjp(forward, *inputs)
        hidden = hidden_f.astype(jnp.bfloat16)
        result = jnp.dot(hidden, out_weight, preferred_element_type=jnp.float32).astype(jnp.bfloat16)
        grad_hidden = jnp.dot(cotangent, out_weight.T, preferred_element_type=jnp.float32)
        grad_q, grad_k, grad_v, grad_g = pull(grad_hidden)
        partial_grad = jnp.dot(hidden.T, cotangent, preferred_element_type=jnp.float32)
        return (result, grad_q.reshape(TIMESTEP_COUNT, HD).astype(jnp.bfloat16), grad_k.reshape(TIMESTEP_COUNT, HD).astype(jnp.bfloat16), grad_v.reshape(TIMESTEP_COUNT, HD).astype(jnp.bfloat16), grad_g.astype(jnp.bfloat16), partial_grad)
    result, grad_q, grad_k, grad_v, grad_g, partial_grad = lax.map(one_sequence, (queries, keys, values, gates, log_decay, grad_out))
    grad_weight = lax.optimization_barrier(jnp.sum(partial_grad, axis=0)) / math.sqrt(TOKENS)
    return (result, grad_q, grad_k, grad_v, grad_g, grad_weight)
```

```python
import functools
import math

import jax
import jax.numpy as jnp
from jax import lax
from jax.experimental import pallas as pl
from jax.experimental.pallas import tpu as pltpu
from jax.sharding import Mesh
from jax.sharding import PartitionSpec as P

F32 = jnp.float32
BF16 = jnp.bfloat16
HIGHEST = lax.Precision.HIGHEST
CHUNK = 256
HEAD = 128
VMEM = 56
GROUP = 4
TOP = 16
EXTRA = 16
NN = (((1,), (0,)), ((), ()))
NT = (((1,), (1,)), ((), ()))
TN = (((0,), (0,)), ((), ()))
FSDP = ("y", "core")
SEQ = ("z", "x")


def dot(a, b, dims, precision=None):
    return lax.dot_general(a, b, dims, precision=precision, preferred_element_type=F32)


def causal(shape):
    return lax.broadcasted_iota(jnp.int32, shape, 0) >= lax.broadcasted_iota(jnp.int32, shape, 1)


def params(mib=VMEM):
    return pltpu.CompilerParams(
        dimension_semantics=("arbitrary",), vmem_limit_bytes=mib * 1024 * 1024
    )


def three_parts(x):
    hi = x.astype(BF16)
    mid = (x - hi.astype(F32)).astype(BF16)
    lo = (x - hi.astype(F32) - mid.astype(F32)).astype(BF16)
    return hi, mid, lo


def states_kernel(ld_ref, k_ref, v_ref, row_ref, col_ref, first_ref, own_ref):
    chunks = ld_ref.shape[2] // CHUNK
    lower = jnp.where(causal((CHUNK, CHUNK)), 1.0, 0.0).astype(F32)
    for c in range(chunks):
        t = slice(c * CHUNK, (c + 1) * CHUNK)
        part = ld_ref[0, :, t]
        row_ref[0, :, t] = dot(part, lower, NT, HIGHEST)
        col_ref[0, t, :] = dot(lower, part, NT, HIGHEST)
    for h in range(GROUP):
        w = slice(h * HEAD, (h + 1) * HEAD)
        state, total = None, None
        for c in range(chunks):
            t = slice(c * CHUNK, (c + 1) * CHUNK)
            a = col_ref[0, t, h : h + 1]
            end = a[CHUNK - 1 : CHUNK]
            scaled = (v_ref[t, w].astype(F32) * jnp.exp(end - a)).astype(BF16)
            new = dot(k_ref[t, w], scaled, TN)
            if c == 0:
                state, total = new, end
                first_ref[h] = new.astype(BF16)
            else:
                state, total = state * jnp.exp(end) + new, total + end
        own_ref[h, :HEAD, :] = state.astype(BF16)
        hi, mid, lo = (p.astype(F32) for p in three_parts(total))
        at = lax.broadcasted_iota(jnp.int32, (EXTRA, HEAD), 0)
        rows = jnp.where(at == 0, hi, jnp.where(at == 1, mid, jnp.where(at == 2, lo, 0.0)))
        own_ref[h, HEAD:, :] = rows.astype(BF16)


def scan_kernel(reverse, parts_ref, decay_ref, ordered_ref, out_ref):
    peers = out_ref.shape[0]
    state = jnp.zeros(out_ref.shape[1:], F32)
    for j in reversed(range(peers)) if reverse else range(peers):
        out_ref[j] = state.astype(BF16)
        rows = decay_ref[j, HEAD:, :].astype(F32)
        decay = jnp.exp(rows[0:1] + rows[1:2] + rows[2:3])
        state = state * decay + parts_ref[j, :HEAD, :].astype(F32)


def decays(row_ref, col_ref, h, c):
    t = slice(c * CHUNK, (c + 1) * CHUNK)
    a = col_ref[0, t, h : h + 1]
    row = row_ref[0, h : h + 1, t]
    weights = jnp.exp(jnp.where(causal((CHUNK, CHUNK)), a - row, -1e30))
    return a, weights


def sigmoid(x):
    return 0.5 + 0.5 * jnp.tanh(0.5 * x)


def inner_kernel(q_ref, k_ref, v_ref, row_ref, col_ref, inner_ref, top_ref):
    chunks = q_ref.shape[0] // CHUNK
    for h in range(GROUP):
        w = slice(h * HEAD, (h + 1) * HEAD)
        for c in range(chunks):
            t = slice(c * CHUNK, (c + 1) * CHUNK)
            _, weights = decays(row_ref, col_ref, h, c)
            scores = (dot(q_ref[t, w], k_ref[t, w], NT) * weights).astype(BF16)
            inner = dot(scores, v_ref[t, w], NN)
            inner_ref[t, w] = inner.astype(BF16)
            if c == 0:
                top_ref[:, w] = inner[:TOP]


def carry_kernel(
    inner_ref, top_ref, q_ref, g_ref, col_ref, in_ref, first_ref,
    norm_ref, norm_top_ref, rms_ref, hidden_ref,
):
    chunks = q_ref.shape[0] // CHUNK
    for h in range(GROUP):
        w = slice(h * HEAD, (h + 1) * HEAD)
        state = in_ref[h]
        for c in range(chunks):
            t = slice(c * CHUNK, (c + 1) * CHUNK)
            a = col_ref[0, t, h : h + 1]
            inner = inner_ref[t, w].astype(F32)
            if c == 0:
                inner = jnp.concatenate([top_ref[:, w], inner[TOP:]], axis=0)
            mixed = inner + dot(q_ref[t, w], state, NN) * jnp.exp(a)
            if c + 1 < chunks:
                end = jnp.exp(a[CHUNK - 1 : CHUNK])
                state = (state.astype(F32) * end + first_ref[h].astype(F32)).astype(BF16)
            rms = lax.rsqrt(jnp.mean(mixed * mixed, axis=-1, keepdims=True) + 1e-05)
            normal = mixed * rms
            gate = g_ref[t, w].astype(F32)
            norm_ref[t, w] = normal.astype(BF16)
            if c == 0:
                norm_top_ref[:, w] = normal[:TOP]
            rms_ref[0, t, h : h + 1] = rms
            hidden_ref[t, w] = (normal * (gate * sigmoid(gate))).astype(BF16)


def middle_kernel(
    cot_ref, weight_ref, norm_ref, norm_top_ref, rms_ref, g_ref, q_ref, col_ref,
    gate_ref, dm_ref, dm_low_ref, last_ref, own_ref,
):
    chunks = q_ref.shape[0] // CHUNK
    grad_hidden = dot(cot_ref[...], weight_ref[...], NT)
    for h in range(GROUP):
        w = slice(h * HEAD, (h + 1) * HEAD)
        state = None
        for c in reversed(range(chunks)):
            t = slice(c * CHUNK, (c + 1) * CHUNK)
            gh = grad_hidden[t, w]
            normal = norm_ref[t, w].astype(F32)
            if c == 0:
                normal = jnp.concatenate([norm_top_ref[:, w], normal[TOP:]], axis=0)
            gate = g_ref[t, w].astype(F32)
            open_part = sigmoid(gate)
            silu = gate * open_part
            slope = open_part + silu - silu * open_part
            gate_ref[t, w] = (gh * normal * slope).astype(BF16)
            dn = gh * silu
            dm = rms_ref[0, t, h : h + 1] * (
                dn - normal * jnp.mean(dn * normal, axis=-1, keepdims=True)
            )
            high = dm.astype(BF16)
            dm_ref[t, w] = high
            if c == 0:
                dm_low_ref[:, w] = (dm[:TOP] - high[:TOP].astype(F32)).astype(BF16)
            a = col_ref[0, t, h : h + 1]
            new = dot(q_ref[t, w], (dm * jnp.exp(a)).astype(BF16), TN)
            if state is None:
                state = new
                last_ref[h] = new.astype(BF16)
            else:
                state = state * jnp.exp(a[CHUNK - 1 : CHUNK]) + new
        own_ref[h] = state.astype(BF16)


def backward_kernel(
    q_ref, k_ref, v_ref, dm_ref, dm_low_ref, row_ref, col_ref, in_ref, first_ref, ordered_ref,
    dq_ref, dk_ref, dv_ref,
):
    chunks = q_ref.shape[0] // CHUNK
    for h in range(GROUP):
        w = slice(h * HEAD, (h + 1) * HEAD)
        state = in_ref[h]
        for c in range(chunks):
            t = slice(c * CHUNK, (c + 1) * CHUNK)
            a, weights = decays(row_ref, col_ref, h, c)
            q, k, v, dm = q_ref[t, w], k_ref[t, w], v_ref[t, w], dm_ref[t, w]
            scores = (dot(q, k, NT) * weights).astype(BF16)
            ds = dot(dm, v, NT)
            if c == 0:
                ds = jnp.concatenate([ds[:TOP] + dot(dm_low_ref[:, w], v, NT), ds[TOP:]], axis=0)
            ds = (ds * weights).astype(BF16)
            dq = dot(ds, k, NN) + dot(dm, state, NT) * jnp.exp(a)
            dq_ref[t, w] = dq.astype(BF16)
            dk_ref[t, w] = dot(ds, q, TN).astype(BF16)
            dv_ref[t, w] = dot(scores, dm, TN).astype(BF16)
            if c + 1 < chunks:
                end = jnp.exp(a[CHUNK - 1 : CHUNK])
                state = (state.astype(F32) * end + first_ref[h].astype(F32)).astype(BF16)


def output_kernel(hidden_ref, weight_ref, ordered_ref, out_ref):
    out_ref[...] = dot(hidden_ref[...], weight_ref[...], NN).astype(BF16)


def finish_kernel(k_ref, v_ref, pk_ref, pv_ref, col_ref, ret_ref, last_ref, dk_ref, dv_ref):
    chunks = k_ref.shape[0] // CHUNK
    for h in range(GROUP):
        w = slice(h * HEAD, (h + 1) * HEAD)
        state = ret_ref[h]
        for c in reversed(range(chunks)):
            t = slice(c * CHUNK, (c + 1) * CHUNK)
            a = col_ref[0, t, h : h + 1]
            end = a[CHUNK - 1 : CHUNK]
            tail = jnp.exp(end - a)
            dk = pk_ref[t, w].astype(F32) + dot(v_ref[t, w], state, NT) * tail
            dv = pv_ref[t, w].astype(F32) + dot(k_ref[t, w], state, NN) * tail
            dk_ref[t, w] = dk.astype(BF16)
            dv_ref[t, w] = dv.astype(BF16)
            if c > 0:
                state = (state.astype(F32) * jnp.exp(end) + last_ref[h].astype(F32)).astype(BF16)


def shards(queries, keys, values, gates, log_decay, out_weight, grad_out):
    length, width = queries.shape[1:]
    heads = log_decay.shape[1]
    groups = heads // GROUP
    q, k, v, g, cot = (a[0] for a in (queries, keys, values, gates, grad_out))
    ld = log_decay[0].reshape(groups, GROUP, length)

    wide = pl.BlockSpec((length, GROUP * HEAD), lambda i: (0, i))
    top = pl.BlockSpec((TOP, GROUP * HEAD), lambda i: (0, i))
    row = pl.BlockSpec((1, GROUP, length), lambda i: (i, 0, 0))
    col = pl.BlockSpec((1, length, GROUP), lambda i: (i, 0, 0))
    mat = pl.BlockSpec((GROUP, HEAD, HEAD), lambda i: (i, 0, 0))
    message = pl.BlockSpec((GROUP, HEAD + EXTRA, HEAD), lambda i: (i, 0, 0))
    wide_t = jax.ShapeDtypeStruct((length, width), BF16)
    top_f = jax.ShapeDtypeStruct((TOP, width), F32)
    top_t = jax.ShapeDtypeStruct((TOP, width), BF16)
    row_t = jax.ShapeDtypeStruct((groups, GROUP, length), F32)
    col_t = jax.ShapeDtypeStruct((groups, length, GROUP), F32)
    mat_t = jax.ShapeDtypeStruct((heads, HEAD, HEAD), BF16)
    message_t = jax.ShapeDtypeStruct((heads, HEAD + EXTRA, HEAD), BF16)

    def call(body, ins, outs, shapes, us=5):
        return pl.pallas_call(
            body,
            grid=(groups,),
            in_specs=ins,
            out_specs=outs,
            out_shape=shapes,
            compiler_params=params(),
            cost_estimate=pl.CostEstimate(
                flops=us * 600_000_000, bytes_accessed=us * 2_500_000, transcendentals=0
            ),
        )

    whole = lax.all_gather(out_weight, FSDP, axis=0, tiled=True)
    a_row, a_col, first, own = call(
        states_kernel, [row, wide, wide], [row, col, mat, message], [row_t, col_t, mat_t, message_t]
    )(ld, k, v)

    anywhere = pl.BlockSpec(memory_space=pl.ANY)
    vmem = pl.BlockSpec(memory_space=pltpu.VMEM)

    def scan(parts, decay, ordered, reverse):
        return pl.pallas_call(
            functools.partial(scan_kernel, reverse),
            in_specs=[vmem, vmem, anywhere],
            out_shape=jax.ShapeDtypeStruct((parts.shape[0], HEAD, HEAD), BF16),
            compiler_params=pltpu.CompilerParams(vmem_limit_bytes=VMEM * 1024 * 1024),
        )(parts, decay, ordered)

    mine = lax.all_to_all(own, SEQ, 0, 0, tiled=True)
    inner, inner_top = call(
        inner_kernel, [wide, wide, wide, row, col], [wide, top], [wide_t, top_f], us=9
    )(q, k, v, a_row, a_col)
    incoming = lax.all_to_all(scan(mine, mine, inner, False), SEQ, 0, 0, tiled=True)

    normal, normal_top, rms, hidden = call(
        carry_kernel,
        [wide, top, wide, wide, col, mat, mat],
        [wide, top, col, wide],
        [wide_t, top_f, col_t, wide_t],
    )(inner, inner_top, q, g, a_col, incoming, first)

    partial_grad = dot(hidden, cot, TN).astype(BF16)
    part = lax.psum_scatter(partial_grad, FSDP, scatter_dimension=0, tiled=True)

    grad_gate, dm, dm_low, last, later = call(
        middle_kernel,
        [
            pl.BlockSpec((length, cot.shape[1]), lambda i: (0, 0)),
            pl.BlockSpec((GROUP * HEAD, cot.shape[1]), lambda i: (i, 0)),
            wide,
            top,
            col,
            wide,
            wide,
            col,
        ],
        [wide, wide, top, mat, mat],
        [wide_t, wide_t, top_t, mat_t, mat_t],
        us=12,
    )(cot, whole, normal, normal_top, rms, g, q, a_col)
    theirs = lax.all_to_all(later, SEQ, 0, 0, tiled=True)
    result = call(
        output_kernel,
        [
            pl.BlockSpec((length, width), lambda i: (0, 0)),
            pl.BlockSpec((width, GROUP * HEAD), lambda i: (0, i)),
            anywhere,
        ],
        wide,
        wide_t,
        us=8,
    )(hidden, whole, later)
    turned = scan(theirs, mine, result, True)
    returning = lax.all_to_all(turned, SEQ, 0, 0, tiled=True)
    grad_q, part_k, part_v = call(
        backward_kernel,
        [wide, wide, wide, wide, top, row, col, mat, mat, anywhere],
        [wide, wide, wide],
        [wide_t, wide_t, wide_t],
        us=13,
    )(q, k, v, dm, dm_low, a_row, a_col, incoming, first, turned)
    grad_k, grad_v = call(
        finish_kernel, [wide, wide, wide, wide, col, mat, mat], [wide, wide], [wide_t, wide_t]
    )(k, v, part_k, part_v, a_col, returning, last)

    peers = lax.axis_size(SEQ)
    part, _ = lax.optimization_barrier((part, part_k))
    pieces = lax.all_to_all(part, SEQ, 0, 0, tiled=True)
    pieces = pieces.reshape(peers, -1, pieces.shape[1]).astype(F32)
    scale = 1.0 / math.sqrt(length * peers * lax.axis_size(FSDP))
    grad_weight = jnp.sum(pieces, axis=0) * scale
    return (
        result[None],
        grad_q[None],
        grad_k[None],
        grad_v[None],
        grad_gate[None],
        grad_weight,
    )


def solution(mesh):
    cut = Mesh(mesh.devices.reshape(4, 2, 4, 4), FSDP + SEQ)
    tokens = P(FSDP, SEQ, None)
    return jax.shard_map(
        shards,
        mesh=cut,
        in_specs=(tokens, tokens, tokens, tokens, P(FSDP, None, SEQ), P(FSDP, None), tokens),
        out_specs=(tokens, tokens, tokens, tokens, tokens, P(FSDP + SEQ, None)),
        check_vma=False,
    )
```

```python
import functools
import math

import jax
import jax.numpy as jnp
from jax import lax
from jax.experimental import pallas as pl
from jax.experimental.pallas import tpu as pltpu
from jax.sharding import Mesh
from jax.sharding import PartitionSpec as P

F32 = jnp.float32
BF16 = jnp.bfloat16
HIGHEST = lax.Precision.HIGHEST
CHUNK = 256
HEAD = 128
VMEM = 56
GROUP = 4
TOP = 16
EXTRA = 16
NN = (((1,), (0,)), ((), ()))
NT = (((1,), (1,)), ((), ()))
TN = (((0,), (0,)), ((), ()))
FSDP = ("y", "core")
SEQ = ("z", "x")


def dot(a, b, dims, precision=None):
    return lax.dot_general(a, b, dims, precision=precision, preferred_element_type=F32)


def causal(shape):
    return lax.broadcasted_iota(jnp.int32, shape, 0) >= lax.broadcasted_iota(jnp.int32, shape, 1)


def params(mib=VMEM):
    return pltpu.CompilerParams(
        dimension_semantics=("arbitrary",), vmem_limit_bytes=mib * 1024 * 1024
    )


def three_parts(x):
    hi = x.astype(BF16)
    mid = (x - hi.astype(F32)).astype(BF16)
    lo = (x - hi.astype(F32) - mid.astype(F32)).astype(BF16)
    return hi, mid, lo


def states_kernel(ld_ref, k_ref, v_ref, row_ref, col_ref, first_ref, own_ref):
    chunks = ld_ref.shape[2] // CHUNK
    step = pl.program_id(0)
    pair = pl.ds(pl.multiple_of(step // 2 * 2 * GROUP, 2 * GROUP), 2 * GROUP)
    lower = jnp.where(causal((CHUNK, CHUNK)), 1.0, 0.0).astype(F32)
    for c in range(chunks):
        t = slice(c * CHUNK, (c + 1) * CHUNK)
        both = ld_ref[0, pair, t]
        part = jnp.where(step % 2 == 0, both[:GROUP], both[GROUP:])
        row_ref[0, :, t] = dot(part, lower, NT, HIGHEST)
        col_ref[0, t, :] = dot(lower, part, NT, HIGHEST)
    for h in range(GROUP):
        w = slice(h * HEAD, (h + 1) * HEAD)
        state, total = None, None
        for c in range(chunks):
            t = slice(c * CHUNK, (c + 1) * CHUNK)
            a = col_ref[0, t, h : h + 1]
            end = a[CHUNK - 1 : CHUNK]
            scaled = (v_ref[t, w].astype(F32) * jnp.exp(end - a)).astype(BF16)
            new = dot(k_ref[t, w], scaled, TN)
            if c == 0:
                state, total = new, end
                first_ref[h] = new.astype(BF16)
            else:
                state, total = state * jnp.exp(end) + new, total + end
        own_ref[h, :HEAD, :] = state.astype(BF16)
        hi, mid, lo = (p.astype(F32) for p in three_parts(total))
        at = lax.broadcasted_iota(jnp.int32, (EXTRA, HEAD), 0)
        rows = jnp.where(at == 0, hi, jnp.where(at == 1, mid, jnp.where(at == 2, lo, 0.0)))
        own_ref[h, HEAD:, :] = rows.astype(BF16)


def scan_kernel(reverse, parts_ref, decay_ref, ordered_ref, out_ref):
    peers = out_ref.shape[0]
    state = jnp.zeros(out_ref.shape[1:], F32)
    for j in reversed(range(peers)) if reverse else range(peers):
        out_ref[j] = state.astype(BF16)
        rows = decay_ref[j, HEAD:, :].astype(F32)
        decay = jnp.exp(rows[0:1] + rows[1:2] + rows[2:3])
        state = state * decay + parts_ref[j, :HEAD, :].astype(F32)


def decays(row_ref, col_ref, h, c):
    t = slice(c * CHUNK, (c + 1) * CHUNK)
    a = col_ref[0, t, h : h + 1]
    row = row_ref[0, h : h + 1, t]
    weights = jnp.exp(jnp.where(causal((CHUNK, CHUNK)), a - row, -1e30))
    return a, weights


def sigmoid(x):
    return 0.5 + 0.5 * jnp.tanh(0.5 * x)


def inner_kernel(
    q_ref, k_ref, v_ref, g_ref, row_ref, col_ref, inner_ref, top_ref, silu_ref
):
    chunks = q_ref.shape[0] // CHUNK
    for h in range(GROUP):
        w = slice(h * HEAD, (h + 1) * HEAD)
        for c in range(chunks):
            t = slice(c * CHUNK, (c + 1) * CHUNK)
            _, weights = decays(row_ref, col_ref, h, c)
            scores = (dot(q_ref[t, w], k_ref[t, w], NT) * weights).astype(BF16)
            gate = g_ref[t, w].astype(F32)
            silu_ref[t, w] = (gate * sigmoid(gate)).astype(BF16)
            inner = dot(scores, v_ref[t, w], NN)
            inner_ref[t, w] = inner.astype(BF16)
            if c == 0:
                top_ref[:, w] = inner[:TOP]


def carry_kernel(
    inner_ref, top_ref, q_ref, silu_ref, col_ref, in_ref, first_ref, cot_ref,
    norm_ref, norm_top_ref, rms_ref, hidden_ref, partial_ref,
):
    chunks = q_ref.shape[0] // CHUNK
    for h in range(GROUP):
        w = slice(h * HEAD, (h + 1) * HEAD)
        state = in_ref[h]
        for c in range(chunks):
            t = slice(c * CHUNK, (c + 1) * CHUNK)
            a = col_ref[0, t, h : h + 1]
            inner = inner_ref[t, w].astype(F32)
            if c == 0:
                inner = jnp.concatenate([top_ref[:, w], inner[TOP:]], axis=0)
            mixed = inner + dot(q_ref[t, w], state, NN) * jnp.exp(a)
            if c + 1 < chunks:
                end = jnp.exp(a[CHUNK - 1 : CHUNK])
                state = (state.astype(F32) * end + first_ref[h].astype(F32)).astype(BF16)
            rms = lax.rsqrt(jnp.mean(mixed * mixed, axis=-1, keepdims=True) + 1e-05)
            normal = mixed * rms
            norm_ref[t, w] = normal.astype(BF16)
            if c == 0:
                norm_top_ref[:, w] = normal[:TOP]
            rms_ref[0, t, h : h + 1] = rms
            hidden_ref[t, w] = (normal * silu_ref[t, w].astype(F32)).astype(BF16)
        if h % 2 == 1:
            pair = slice((h - 1) * HEAD, (h + 1) * HEAD)
            partial_ref[pair, :] = dot(hidden_ref[:, pair], cot_ref[...], TN).astype(BF16)


def middle_kernel(
    cot_ref, weight_ref, norm_ref, norm_top_ref, rms_ref, g_ref, q_ref, col_ref,
    gate_ref, dm_ref, dm_low_ref, last_ref, own_ref,
):
    chunks = q_ref.shape[0] // CHUNK
    grad_hidden = dot(cot_ref[...], weight_ref[...], NT)
    for h in range(GROUP):
        w = slice(h * HEAD, (h + 1) * HEAD)
        state = None
        for c in reversed(range(chunks)):
            t = slice(c * CHUNK, (c + 1) * CHUNK)
            gh = grad_hidden[t, w]
            normal = norm_ref[t, w].astype(F32)
            if c == 0:
                normal = jnp.concatenate([norm_top_ref[:, w], normal[TOP:]], axis=0)
            gate = g_ref[t, w].astype(F32)
            open_part = sigmoid(gate)
            silu = gate * open_part
            slope = open_part + silu - silu * open_part
            gate_ref[t, w] = (gh * normal * slope).astype(BF16)
            dn = gh * silu
            dm = rms_ref[0, t, h : h + 1] * (
                dn - normal * jnp.mean(dn * normal, axis=-1, keepdims=True)
            )
            high = dm.astype(BF16)
            dm_ref[t, w] = high
            if c == 0:
                dm_low_ref[:, w] = (dm[:TOP] - high[:TOP].astype(F32)).astype(BF16)
            a = col_ref[0, t, h : h + 1]
            new = dot(q_ref[t, w], (dm * jnp.exp(a)).astype(BF16), TN)
            if state is None:
                state = new
                last_ref[h] = new.astype(BF16)
            else:
                state = state * jnp.exp(a[CHUNK - 1 : CHUNK]) + new
        own_ref[h] = state.astype(BF16)


def backward_kernel(
    q_ref, k_ref, v_ref, dm_ref, dm_low_ref, row_ref, col_ref, in_ref, first_ref, ordered_ref,
    dq_ref, dk_ref, dv_ref,
):
    chunks = q_ref.shape[0] // CHUNK
    for h in range(GROUP):
        w = slice(h * HEAD, (h + 1) * HEAD)
        state = in_ref[h]
        for c in range(chunks):
            t = slice(c * CHUNK, (c + 1) * CHUNK)
            a, weights = decays(row_ref, col_ref, h, c)
            q, k, v, dm = q_ref[t, w], k_ref[t, w], v_ref[t, w], dm_ref[t, w]
            scores = (dot(q, k, NT) * weights).astype(BF16)
            ds = dot(dm, v, NT)
            if c == 0:
                ds = jnp.concatenate([ds[:TOP] + dot(dm_low_ref[:, w], v, NT), ds[TOP:]], axis=0)
            ds = (ds * weights).astype(BF16)
            dq = dot(ds, k, NN) + dot(dm, state, NT) * jnp.exp(a)
            dq_ref[t, w] = dq.astype(BF16)
            dk_ref[t, w] = dot(ds, q, TN).astype(BF16)
            dv_ref[t, w] = dot(scores, dm, TN).astype(BF16)
            if c + 1 < chunks:
                end = jnp.exp(a[CHUNK - 1 : CHUNK])
                state = (state.astype(F32) * end + first_ref[h].astype(F32)).astype(BF16)


def output_kernel(hidden_ref, weight_ref, ordered_ref, out_ref):
    out_ref[...] = dot(hidden_ref[...], weight_ref[...], NN).astype(BF16)


def finish_kernel(k_ref, v_ref, pk_ref, pv_ref, col_ref, ret_ref, last_ref, dk_ref, dv_ref):
    chunks = k_ref.shape[0] // CHUNK
    for h in range(GROUP):
        w = slice(h * HEAD, (h + 1) * HEAD)
        state = ret_ref[h]
        for c in reversed(range(chunks)):
            t = slice(c * CHUNK, (c + 1) * CHUNK)
            a = col_ref[0, t, h : h + 1]
            end = a[CHUNK - 1 : CHUNK]
            tail = jnp.exp(end - a)
            dk = pk_ref[t, w].astype(F32) + dot(v_ref[t, w], state, NT) * tail
            dv = pv_ref[t, w].astype(F32) + dot(k_ref[t, w], state, NN) * tail
            dk_ref[t, w] = dk.astype(BF16)
            dv_ref[t, w] = dv.astype(BF16)
            if c > 0:
                state = (state.astype(F32) * jnp.exp(end) + last_ref[h].astype(F32)).astype(BF16)


def shards(queries, keys, values, gates, log_decay, out_weight, grad_out):
    length, width = queries.shape[1:]
    heads = log_decay.shape[1]
    groups = heads // GROUP
    q, k, v, g, cot = (a[0] for a in (queries, keys, values, gates, grad_out))

    wide = pl.BlockSpec((length, GROUP * HEAD), lambda i: (0, i))
    all_decays = pl.BlockSpec((1, heads, length), lambda i: (0, 0, 0))
    top = pl.BlockSpec((TOP, GROUP * HEAD), lambda i: (0, i))
    row = pl.BlockSpec((1, GROUP, length), lambda i: (i, 0, 0))
    col = pl.BlockSpec((1, length, GROUP), lambda i: (i, 0, 0))
    mat = pl.BlockSpec((GROUP, HEAD, HEAD), lambda i: (i, 0, 0))
    message = pl.BlockSpec((GROUP, HEAD + EXTRA, HEAD), lambda i: (i, 0, 0))
    wide_t = jax.ShapeDtypeStruct((length, width), BF16)
    top_f = jax.ShapeDtypeStruct((TOP, width), F32)
    top_t = jax.ShapeDtypeStruct((TOP, width), BF16)
    row_t = jax.ShapeDtypeStruct((groups, GROUP, length), F32)
    col_t = jax.ShapeDtypeStruct((groups, length, GROUP), F32)
    mat_t = jax.ShapeDtypeStruct((heads, HEAD, HEAD), BF16)
    message_t = jax.ShapeDtypeStruct((heads, HEAD + EXTRA, HEAD), BF16)

    def call(body, ins, outs, shapes, us=5):
        return pl.pallas_call(
            body,
            grid=(groups,),
            in_specs=ins,
            out_specs=outs,
            out_shape=shapes,
            compiler_params=params(),
            cost_estimate=pl.CostEstimate(
                flops=us * 600_000_000, bytes_accessed=us * 2_500_000, transcendentals=0
            ),
        )

    whole = lax.all_gather(out_weight, FSDP, axis=0, tiled=True)
    a_row, a_col, first, own = call(
        states_kernel, [all_decays, wide, wide], [row, col, mat, message], [row_t, col_t, mat_t, message_t]
    )(log_decay, k, v)

    anywhere = pl.BlockSpec(memory_space=pl.ANY)
    vmem = pl.BlockSpec(memory_space=pltpu.VMEM)

    def scan(parts, decay, ordered, reverse):
        return pl.pallas_call(
            functools.partial(scan_kernel, reverse),
            in_specs=[vmem, vmem, anywhere],
            out_shape=jax.ShapeDtypeStruct((parts.shape[0], HEAD, HEAD), BF16),
            compiler_params=pltpu.CompilerParams(vmem_limit_bytes=VMEM * 1024 * 1024),
        )(parts, decay, ordered)

    mine = lax.all_to_all(own, SEQ, 0, 0, tiled=True)
    inner, inner_top, silu = call(
        inner_kernel,
        [wide, wide, wide, wide, row, col],
        [wide, top, wide],
        [wide_t, top_f, wide_t],
        us=9,
    )(q, k, v, g, a_row, a_col)
    incoming = lax.all_to_all(scan(mine, mine, inner, False), SEQ, 0, 0, tiled=True)

    normal, normal_top, rms, hidden, partial_grad = call(
        carry_kernel,
        [wide, top, wide, wide, col, mat, mat, pl.BlockSpec(cot.shape, lambda i: (0, 0))],
        [wide, top, col, wide, pl.BlockSpec((GROUP * HEAD, cot.shape[1]), lambda i: (i, 0))],
        [
            wide_t,
            top_f,
            col_t,
            wide_t,
            jax.ShapeDtypeStruct((width, cot.shape[1]), BF16),
        ],
        us=12,
    )(inner, inner_top, q, silu, a_col, incoming, first, cot)

    part = lax.psum_scatter(partial_grad, FSDP, scatter_dimension=0, tiled=True)

    grad_gate, dm, dm_low, last, later = call(
        middle_kernel,
        [
            pl.BlockSpec((length, cot.shape[1]), lambda i: (0, 0)),
            pl.BlockSpec((GROUP * HEAD, cot.shape[1]), lambda i: (i, 0)),
            wide,
            top,
            col,
            wide,
            wide,
            col,
        ],
        [wide, wide, top, mat, mat],
        [wide_t, wide_t, top_t, mat_t, mat_t],
        us=12,
    )(cot, whole, normal, normal_top, rms, g, q, a_col)
    theirs = lax.all_to_all(later, SEQ, 0, 0, tiled=True)
    result = call(
        output_kernel,
        [
            pl.BlockSpec((length, width), lambda i: (0, 0)),
            pl.BlockSpec((width, GROUP * HEAD), lambda i: (0, i)),
            anywhere,
        ],
        wide,
        wide_t,
        us=8,
    )(hidden, whole, later)
    turned = scan(theirs, mine, result, True)
    returning = lax.all_to_all(turned, SEQ, 0, 0, tiled=True)
    grad_q, part_k, part_v = call(
        backward_kernel,
        [wide, wide, wide, wide, top, row, col, mat, mat, anywhere],
        [wide, wide, wide],
        [wide_t, wide_t, wide_t],
        us=13,
    )(q, k, v, dm, dm_low, a_row, a_col, incoming, first, turned)
    grad_k, grad_v = call(
        finish_kernel, [wide, wide, wide, wide, col, mat, mat], [wide, wide], [wide_t, wide_t]
    )(k, v, part_k, part_v, a_col, returning, last)

    peers = lax.axis_size(SEQ)
    part, _ = lax.optimization_barrier((part, part_k))
    pieces = lax.all_to_all(part, SEQ, 0, 0, tiled=True)
    pieces = pieces.reshape(peers, -1, pieces.shape[1]).astype(F32)
    scale = 1.0 / math.sqrt(length * peers * lax.axis_size(FSDP))
    grad_weight = jnp.sum(pieces, axis=0) * scale
    return (
        result[None],
        grad_q[None],
        grad_k[None],
        grad_v[None],
        grad_gate[None],
        grad_weight,
    )


def solution(mesh):
    cut = Mesh(mesh.devices.reshape(4, 2, 4, 4), FSDP + SEQ)
    tokens = P(FSDP, SEQ, None)
    return jax.shard_map(
        shards,
        mesh=cut,
        in_specs=(tokens, tokens, tokens, tokens, P(FSDP, None, SEQ), P(FSDP, None), tokens),
        out_specs=(tokens, tokens, tokens, tokens, tokens, P(FSDP + SEQ, None)),
        check_vma=False,
    )
```

```python
import functools
import math

import jax
import jax.numpy as jnp
from jax import lax
from jax.experimental import pallas as pl
from jax.experimental.pallas import tpu as pltpu
from jax.sharding import Mesh
from jax.sharding import PartitionSpec as P

F32 = jnp.float32
BF16 = jnp.bfloat16
HIGHEST = lax.Precision.HIGHEST
CHUNK = 256
HEAD = 128
VMEM = 56
GROUP = 4
TOP = 16
EXTRA = 16
NN = (((1,), (0,)), ((), ()))
NT = (((1,), (1,)), ((), ()))
TN = (((0,), (0,)), ((), ()))
FSDP = ("y", "core")
SEQ = ("z", "x")


def dot(a, b, dims, precision=None):
    return lax.dot_general(a, b, dims, precision=precision, preferred_element_type=F32)


def causal(shape):
    return lax.broadcasted_iota(jnp.int32, shape, 0) >= lax.broadcasted_iota(jnp.int32, shape, 1)


def params(mib=VMEM):
    return pltpu.CompilerParams(
        dimension_semantics=("arbitrary",), vmem_limit_bytes=mib * 1024 * 1024
    )


def three_parts(x):
    hi = x.astype(BF16)
    mid = (x - hi.astype(F32)).astype(BF16)
    lo = (x - hi.astype(F32) - mid.astype(F32)).astype(BF16)
    return hi, mid, lo


def states_kernel(ld_ref, k_ref, v_ref, row_ref, col_ref, first_ref, own_ref):
    chunks = ld_ref.shape[2] // CHUNK
    step = pl.program_id(0)
    pair = pl.ds(pl.multiple_of(step // 2 * 2 * GROUP, 2 * GROUP), 2 * GROUP)
    lower = jnp.where(causal((CHUNK, CHUNK)), 1.0, 0.0).astype(F32)
    for c in range(chunks):
        t = slice(c * CHUNK, (c + 1) * CHUNK)
        both = ld_ref[0, pair, t]
        part = jnp.where(step % 2 == 0, both[:GROUP], both[GROUP:])
        row_ref[0, :, t] = dot(part, lower, NT, HIGHEST)
        col_ref[0, t, :] = dot(lower, part, NT, HIGHEST)
    for h in range(GROUP):
        w = slice(h * HEAD, (h + 1) * HEAD)
        state, total = None, None
        for c in range(chunks):
            t = slice(c * CHUNK, (c + 1) * CHUNK)
            a = col_ref[0, t, h : h + 1]
            end = a[CHUNK - 1 : CHUNK]
            scaled = (v_ref[t, w].astype(F32) * jnp.exp(end - a)).astype(BF16)
            new = dot(k_ref[t, w], scaled, TN)
            if c == 0:
                state, total = new, end
                first_ref[h] = new.astype(BF16)
            else:
                state, total = state * jnp.exp(end) + new, total + end
        own_ref[h, :HEAD, :] = state.astype(BF16)
        hi, mid, lo = (p.astype(F32) for p in three_parts(total))
        at = lax.broadcasted_iota(jnp.int32, (EXTRA, HEAD), 0)
        rows = jnp.where(at == 0, hi, jnp.where(at == 1, mid, jnp.where(at == 2, lo, 0.0)))
        own_ref[h, HEAD:, :] = rows.astype(BF16)


def scan_kernel(reverse, parts_ref, decay_ref, ordered_ref, out_ref):
    peers = out_ref.shape[0]
    state = jnp.zeros(out_ref.shape[1:], F32)
    for j in reversed(range(peers)) if reverse else range(peers):
        out_ref[j] = state.astype(BF16)
        rows = decay_ref[j, HEAD:, :].astype(F32)
        decay = jnp.exp(rows[0:1] + rows[1:2] + rows[2:3])
        state = state * decay + parts_ref[j, :HEAD, :].astype(F32)


def decays(row_ref, col_ref, h, c):
    t = slice(c * CHUNK, (c + 1) * CHUNK)
    a = col_ref[0, t, h : h + 1]
    row = row_ref[0, h : h + 1, t]
    weights = jnp.exp(jnp.where(causal((CHUNK, CHUNK)), a - row, -1e30))
    return a, weights


def sigmoid(x):
    return 0.5 + 0.5 * jnp.tanh(0.5 * x)


def inner_kernel(
    q_ref, k_ref, v_ref, g_ref, row_ref, col_ref, inner_ref, top_ref, silu_ref, faded_ref
):
    chunks = q_ref.shape[0] // CHUNK
    for h in range(GROUP):
        w = slice(h * HEAD, (h + 1) * HEAD)
        for c in range(chunks):
            t = slice(c * CHUNK, (c + 1) * CHUNK)
            a, weights = decays(row_ref, col_ref, h, c)
            faded_ref[t, w] = (q_ref[t, w].astype(F32) * jnp.exp(a)).astype(BF16)
            scores = (dot(q_ref[t, w], k_ref[t, w], NT) * weights).astype(BF16)
            gate = g_ref[t, w].astype(F32)
            silu_ref[t, w] = (gate * sigmoid(gate)).astype(BF16)
            inner = dot(scores, v_ref[t, w], NN)
            inner_ref[t, w] = inner.astype(BF16)
            if c == 0:
                top_ref[:, w] = inner[:TOP]


def carry_kernel(
    inner_ref, top_ref, q_ref, silu_ref, col_ref, in_ref, first_ref, cot_ref,
    norm_ref, norm_top_ref, rms_ref, hidden_ref, partial_ref,
):
    chunks = q_ref.shape[0] // CHUNK
    for h in range(GROUP):
        w = slice(h * HEAD, (h + 1) * HEAD)
        state = in_ref[h]
        for c in range(chunks):
            t = slice(c * CHUNK, (c + 1) * CHUNK)
            a = col_ref[0, t, h : h + 1]
            inner = inner_ref[t, w].astype(F32)
            if c == 0:
                inner = jnp.concatenate([top_ref[:, w], inner[TOP:]], axis=0)
            mixed = inner + dot(q_ref[t, w], state, NN)
            if c + 1 < chunks:
                end = jnp.exp(a[CHUNK - 1 : CHUNK])
                state = (state.astype(F32) * end + first_ref[h].astype(F32)).astype(BF16)
            rms = lax.rsqrt(jnp.mean(mixed * mixed, axis=-1, keepdims=True) + 1e-05)
            normal = mixed * rms
            norm_ref[t, w] = normal.astype(BF16)
            if c == 0:
                norm_top_ref[:, w] = normal[:TOP]
            rms_ref[0, t, h : h + 1] = rms
            hidden_ref[t, w] = (normal * silu_ref[t, w].astype(F32)).astype(BF16)
        if h % 2 == 1:
            pair = slice((h - 1) * HEAD, (h + 1) * HEAD)
            partial_ref[pair, :] = dot(hidden_ref[:, pair], cot_ref[...], TN).astype(BF16)


def middle_kernel(
    cot_ref, weight_ref, norm_ref, norm_top_ref, rms_ref, g_ref, q_ref, col_ref,
    gate_ref, dm_ref, dm_low_ref, last_ref, own_ref,
):
    chunks = q_ref.shape[0] // CHUNK
    grad_hidden = dot(cot_ref[...], weight_ref[...], NT)
    for h in range(GROUP):
        w = slice(h * HEAD, (h + 1) * HEAD)
        state = None
        for c in reversed(range(chunks)):
            t = slice(c * CHUNK, (c + 1) * CHUNK)
            gh = grad_hidden[t, w]
            normal = norm_ref[t, w].astype(F32)
            if c == 0:
                normal = jnp.concatenate([norm_top_ref[:, w], normal[TOP:]], axis=0)
            gate = g_ref[t, w].astype(F32)
            open_part = sigmoid(gate)
            silu = gate * open_part
            slope = open_part + silu - silu * open_part
            gate_ref[t, w] = (gh * normal * slope).astype(BF16)
            dn = gh * silu
            dm = rms_ref[0, t, h : h + 1] * (
                dn - normal * jnp.mean(dn * normal, axis=-1, keepdims=True)
            )
            high = dm.astype(BF16)
            dm_ref[t, w] = high
            if c == 0:
                dm_low_ref[:, w] = (dm[:TOP] - high[:TOP].astype(F32)).astype(BF16)
            a = col_ref[0, t, h : h + 1]
            new = dot(q_ref[t, w], (dm * jnp.exp(a)).astype(BF16), TN)
            if state is None:
                state = new
                last_ref[h] = new.astype(BF16)
            else:
                state = state * jnp.exp(a[CHUNK - 1 : CHUNK]) + new
        own_ref[h] = state.astype(BF16)


def backward_kernel(
    q_ref, k_ref, v_ref, dm_ref, dm_low_ref, row_ref, col_ref, in_ref, first_ref, ordered_ref,
    dq_ref, dk_ref, dv_ref,
):
    chunks = q_ref.shape[0] // CHUNK
    for h in range(GROUP):
        w = slice(h * HEAD, (h + 1) * HEAD)
        state = in_ref[h]
        for c in range(chunks):
            t = slice(c * CHUNK, (c + 1) * CHUNK)
            a, weights = decays(row_ref, col_ref, h, c)
            q, k, v, dm = q_ref[t, w], k_ref[t, w], v_ref[t, w], dm_ref[t, w]
            scores = (dot(q, k, NT) * weights).astype(BF16)
            ds = dot(dm, v, NT)
            if c == 0:
                ds = jnp.concatenate([ds[:TOP] + dot(dm_low_ref[:, w], v, NT), ds[TOP:]], axis=0)
            ds = (ds * weights).astype(BF16)
            dq = dot(ds, k, NN) + dot(dm, state, NT) * jnp.exp(a)
            dq_ref[t, w] = dq.astype(BF16)
            dk_ref[t, w] = dot(ds, q, TN).astype(BF16)
            dv_ref[t, w] = dot(scores, dm, TN).astype(BF16)
            if c + 1 < chunks:
                end = jnp.exp(a[CHUNK - 1 : CHUNK])
                state = (state.astype(F32) * end + first_ref[h].astype(F32)).astype(BF16)


def output_kernel(hidden_ref, weight_ref, ordered_ref, out_ref):
    out_ref[...] = dot(hidden_ref[...], weight_ref[...], NN).astype(BF16)


def finish_kernel(k_ref, v_ref, pk_ref, pv_ref, col_ref, ret_ref, last_ref, dk_ref, dv_ref):
    chunks = k_ref.shape[0] // CHUNK
    for h in range(GROUP):
        w = slice(h * HEAD, (h + 1) * HEAD)
        state = ret_ref[h]
        for c in reversed(range(chunks)):
            t = slice(c * CHUNK, (c + 1) * CHUNK)
            a = col_ref[0, t, h : h + 1]
            end = a[CHUNK - 1 : CHUNK]
            tail = jnp.exp(end - a)
            dk = pk_ref[t, w].astype(F32) + dot(v_ref[t, w], state, NT) * tail
            dv = pv_ref[t, w].astype(F32) + dot(k_ref[t, w], state, NN) * tail
            dk_ref[t, w] = dk.astype(BF16)
            dv_ref[t, w] = dv.astype(BF16)
            if c > 0:
                state = (state.astype(F32) * jnp.exp(end) + last_ref[h].astype(F32)).astype(BF16)


def shards(queries, keys, values, gates, log_decay, out_weight, grad_out):
    length, width = queries.shape[1:]
    heads = log_decay.shape[1]
    groups = heads // GROUP
    q, k, v, g, cot = (a[0] for a in (queries, keys, values, gates, grad_out))

    wide = pl.BlockSpec((length, GROUP * HEAD), lambda i: (0, i))
    all_decays = pl.BlockSpec((1, heads, length), lambda i: (0, 0, 0))
    top = pl.BlockSpec((TOP, GROUP * HEAD), lambda i: (0, i))
    row = pl.BlockSpec((1, GROUP, length), lambda i: (i, 0, 0))
    col = pl.BlockSpec((1, length, GROUP), lambda i: (i, 0, 0))
    mat = pl.BlockSpec((GROUP, HEAD, HEAD), lambda i: (i, 0, 0))
    message = pl.BlockSpec((GROUP, HEAD + EXTRA, HEAD), lambda i: (i, 0, 0))
    wide_t = jax.ShapeDtypeStruct((length, width), BF16)
    top_f = jax.ShapeDtypeStruct((TOP, width), F32)
    top_t = jax.ShapeDtypeStruct((TOP, width), BF16)
    row_t = jax.ShapeDtypeStruct((groups, GROUP, length), F32)
    col_t = jax.ShapeDtypeStruct((groups, length, GROUP), F32)
    mat_t = jax.ShapeDtypeStruct((heads, HEAD, HEAD), BF16)
    message_t = jax.ShapeDtypeStruct((heads, HEAD + EXTRA, HEAD), BF16)

    def call(body, ins, outs, shapes, us=5):
        return pl.pallas_call(
            body,
            grid=(groups,),
            in_specs=ins,
            out_specs=outs,
            out_shape=shapes,
            compiler_params=params(),
            cost_estimate=pl.CostEstimate(
                flops=us * 600_000_000, bytes_accessed=us * 2_500_000, transcendentals=0
            ),
        )

    whole = lax.all_gather(out_weight, FSDP, axis=0, tiled=True)
    a_row, a_col, first, own = call(
        states_kernel, [all_decays, wide, wide], [row, col, mat, message], [row_t, col_t, mat_t, message_t]
    )(log_decay, k, v)

    anywhere = pl.BlockSpec(memory_space=pl.ANY)
    vmem = pl.BlockSpec(memory_space=pltpu.VMEM)

    def scan(parts, decay, ordered, reverse):
        return pl.pallas_call(
            functools.partial(scan_kernel, reverse),
            in_specs=[vmem, vmem, anywhere],
            out_shape=jax.ShapeDtypeStruct((parts.shape[0], HEAD, HEAD), BF16),
            compiler_params=pltpu.CompilerParams(vmem_limit_bytes=VMEM * 1024 * 1024),
        )(parts, decay, ordered)

    mine = lax.all_to_all(own, SEQ, 0, 0, tiled=True)
    inner, inner_top, silu, faded = call(
        inner_kernel,
        [wide, wide, wide, wide, row, col],
        [wide, top, wide, wide],
        [wide_t, top_f, wide_t, wide_t],
        us=9,
    )(q, k, v, g, a_row, a_col)
    incoming = lax.all_to_all(scan(mine, mine, inner, False), SEQ, 0, 0, tiled=True)

    normal, normal_top, rms, hidden, partial_grad = call(
        carry_kernel,
        [wide, top, wide, wide, col, mat, mat, pl.BlockSpec(cot.shape, lambda i: (0, 0))],
        [wide, top, col, wide, pl.BlockSpec((GROUP * HEAD, cot.shape[1]), lambda i: (i, 0))],
        [
            wide_t,
            top_f,
            col_t,
            wide_t,
            jax.ShapeDtypeStruct((width, cot.shape[1]), BF16),
        ],
        us=12,
    )(inner, inner_top, faded, silu, a_col, incoming, first, cot)

    part = lax.psum_scatter(partial_grad, FSDP, scatter_dimension=0, tiled=True)

    grad_gate, dm, dm_low, last, later = call(
        middle_kernel,
        [
            pl.BlockSpec((length, cot.shape[1]), lambda i: (0, 0)),
            pl.BlockSpec((GROUP * HEAD, cot.shape[1]), lambda i: (i, 0)),
            wide,
            top,
            col,
            wide,
            wide,
            col,
        ],
        [wide, wide, top, mat, mat],
        [wide_t, wide_t, top_t, mat_t, mat_t],
        us=12,
    )(cot, whole, normal, normal_top, rms, g, q, a_col)
    theirs = lax.all_to_all(later, SEQ, 0, 0, tiled=True)
    result = call(
        output_kernel,
        [
            pl.BlockSpec((length, width), lambda i: (0, 0)),
            pl.BlockSpec((width, GROUP * HEAD), lambda i: (0, i)),
            anywhere,
        ],
        wide,
        wide_t,
        us=8,
    )(hidden, whole, later)
    turned = scan(theirs, mine, result, True)
    returning = lax.all_to_all(turned, SEQ, 0, 0, tiled=True)
    grad_q, part_k, part_v = call(
        backward_kernel,
        [wide, wide, wide, wide, top, row, col, mat, mat, anywhere],
        [wide, wide, wide],
        [wide_t, wide_t, wide_t],
        us=13,
    )(q, k, v, dm, dm_low, a_row, a_col, incoming, first, turned)
    grad_k, grad_v = call(
        finish_kernel, [wide, wide, wide, wide, col, mat, mat], [wide, wide], [wide_t, wide_t]
    )(k, v, part_k, part_v, a_col, returning, last)

    peers = lax.axis_size(SEQ)
    part, _ = lax.optimization_barrier((part, part_k))
    pieces = lax.all_to_all(part, SEQ, 0, 0, tiled=True)
    pieces = pieces.reshape(peers, -1, pieces.shape[1]).astype(F32)
    scale = 1.0 / math.sqrt(length * peers * lax.axis_size(FSDP))
    grad_weight = jnp.sum(pieces, axis=0) * scale
    return (
        result[None],
        grad_q[None],
        grad_k[None],
        grad_v[None],
        grad_gate[None],
        grad_weight,
    )


def solution(mesh):
    cut = Mesh(mesh.devices.reshape(4, 2, 4, 4), FSDP + SEQ)
    tokens = P(FSDP, SEQ, None)
    return jax.shard_map(
        shards,
        mesh=cut,
        in_specs=(tokens, tokens, tokens, tokens, P(FSDP, None, SEQ), P(FSDP, None), tokens),
        out_specs=(tokens, tokens, tokens, tokens, tokens, P(FSDP + SEQ, None)),
        check_vma=False,
    )
```
